128 devices in a mesh: row: 16 (over y, z_hi, core), col: 8 (over z_lo, x).
Axes of the slice: x: 4, y: 4, z: 4 (z_hi: 2, z_lo: 2; z = z_hi * 2 + z_lo), core: 2. Of those that a mesh axis runs over, the one named last changes fastest.
Arguments:
- features_in: bfloat16 [65536, 256], P(('row', 'col')), may hold values from -6 to 6
- weight: bfloat16 [256, 256], replicated, may hold values from -0.375 to 0.375
- bias_vector: float32 [256], replicated, may hold values from -3 to 3
- cotangent: bfloat16 [65536, 256], P(('row', 'col')), may hold values from -6 to 6
- adjacency: bfloat16 [16, 8, 512, 128, 128], P('row', 'col'), may hold values from -0.0625 to 0.0625
- block_rows: int32 [16, 8, 512], P('row', 'col'), may hold values from 0 to 31, as said below
- block_cols: int32 [16, 8, 512], P('row', 'col'), may hold values from 0 to 63, as said below
- counts: int32 [16, 8], P('row', 'col'), may hold values from 64 to 512, as said below
Outputs:
- output: bfloat16 [65536, 256], P(('row', 'col'))
- grad_x: bfloat16 [65536, 256], P(('row', 'col'))
- grad_w: float32 [256, 256], replicated
The draws below stay inside these ranges and needn't reach their ends.
Inputs may be any that keep to these rules, and one draw needn't show every extreme that they name: Within one tile the pairs (block_rows, block_cols) of all 512 slots are distinct. `block_cols`: pairs with block_rows as stated there. `counts`: slots at or past a tile's count are not part of A. Some tile has exactly 512 live slots.
All inputs are finite; a program needn't handle non-finite values.
Results may differ from the reference program's by a relative error of at most 0.025.
Values may be sent and summed in bfloat16 or wider, within the bound.
No kernel may reach another device: no remote copies, remote signals or barrier semaphores. Data moves between devices by JAX's collectives and lax.ppermute only.
A program may use at most 192 MiB of HBM per device.

```python
import math
import jax
import jax.numpy as jnp
from jax import lax

F = 256
BLOCK = 128
NODE_DEV = 512
NODES = 65536
ROW_BLOCKS = 32
COL_BLOCKS = 64
SLOTS = 512
N_ROW = 16
N_COL = 8


def slot_positions(key):
    inner = jax.random.fold_in(key, 7)
    tile_keys = jax.random.split(inner, N_ROW * N_COL)
    chosen = jax.vmap(lambda tile_key: jax.random.permutation(tile_key, ROW_BLOCKS * COL_BLOCKS)[:SLOTS])(tile_keys)
    return chosen.astype(jnp.int32).reshape(N_ROW, N_COL, SLOTS)


def draw_block_rows(key, part):
    positions = slot_positions(key)
    return (positions // COL_BLOCKS).astype(jnp.int32)


def draw_block_cols(key, part):
    positions = slot_positions(key)
    return (positions % COL_BLOCKS).astype(jnp.int32)


def draw_counts(key, part):
    key = jax.random.fold_in(key, 3)
    shift_key, full_key = jax.random.split(key)
    shifts = jax.random.randint(shift_key, (N_ROW * N_COL,), 0, 4)
    values = jnp.right_shift(jnp.full((N_ROW * N_COL,), SLOTS, jnp.int32), shifts.astype(jnp.int32))
    full_tile = jax.random.randint(full_key, (), 0, N_ROW * N_COL)
    values = values.at[full_tile].set(SLOTS)
    return values.astype(jnp.int32).reshape(N_ROW, N_COL)


def block_scale(key, dims, cuts, low, largest):
    factor_of, own = 1.0, jax.random.fold_in(key, 6)
    for axis_at, blocks in cuts:
        draws = jnp.exp(jax.random.uniform(jax.random.fold_in(own, axis_at), (blocks,), jnp.float32, low / len(cuts), largest / len(cuts)))
        factor_of = factor_of * jnp.repeat(draws, dims[axis_at] // blocks).reshape([-1 if axis == axis_at else 1 for axis in range(len(dims))])
    return factor_of


def bell_draw(own_key, extent, width, most, cuts=(), kind=jnp.bfloat16):
    loudness = block_scale(own_key, extent, cuts, -0.22, 0.18) if cuts else 1.0
    array = jax.random.normal(own_key, extent, jnp.float32) * width * loudness
    return jnp.minimum(jnp.maximum(array, -most), most).astype(kind)


def setup_inputs(seed: int = 0) -> dict:
    splits = jax.random.split(jax.random.key(seed), 9)
    features_in = bell_draw(splits[0], (NODES, F), 1.0, 6.0, ((0, 128),))
    weight = bell_draw(splits[1], (F, F), F ** -0.5, 0.375)
    bias_vector = bell_draw(splits[2], (F,), 0.5, 3.0, (), jnp.float32)
    cotangent = bell_draw(splits[3], (NODES, F), 1.0, 6.0, ((0, 128),))
    adjacency = bell_draw(splits[4], (N_ROW, N_COL, SLOTS, BLOCK, BLOCK), (SLOTS * BLOCK * N_COL // (2 * ROW_BLOCKS)) ** -0.5, 0.0625, ((0, 16), (1, 8)))
    block_rows = draw_block_rows(jax.random.fold_in(splits[8], 71), 0)
    block_cols = draw_block_cols(jax.random.fold_in(splits[8], 71), 0)
    counts = draw_counts(jax.random.fold_in(splits[8], 71), 0)
    return {"features_in": features_in, "weight": weight, "bias_vector": bias_vector, "cotangent": cotangent, "adjacency": adjacency, "block_rows": block_rows, "block_cols": block_cols, "counts": counts}


def silu_slope(value):
    sigmoid_v = jax.nn.sigmoid(value)
    return sigmoid_v * (1.0 + value * (1.0 - sigmoid_v))

def reference(features_in, weight, bias_vector, cotangent, adjacency, block_rows, block_cols, counts):
    nodes_all = features_in.shape[0]
    feature_width = features_in.shape[1]
    hidden_in = jnp.dot(features_in, weight, preferred_element_type=jnp.float32).astype(jnp.bfloat16)
    column_sets = hidden_in.reshape(N_ROW, N_COL, NODE_DEV, feature_width)
    slot_ids = jnp.arange(SLOTS, dtype=jnp.int32)
    row_ids = jnp.arange(ROW_BLOCKS, dtype=jnp.int32)
    col_ids = jnp.arange(COL_BLOCKS, dtype=jnp.int32)

    def forward_block_pass(tile_index, totals):
        row_part = (tile_index // N_COL).astype(jnp.int32)
        col_part = (tile_index % N_COL).astype(jnp.int32)
        column_set = lax.dynamic_index_in_dim(column_sets, col_part, 1, keepdims=False)
        column_set = column_set.reshape(COL_BLOCKS, BLOCK, feature_width)
        tile_blocks = adjacency[row_part, col_part]
        rows_here = block_rows[row_part, col_part]
        cols_here = block_cols[row_part, col_part]
        is_live = slot_ids < counts[row_part, col_part]
        gathered = jnp.take(column_set, cols_here, axis=0)
        block_products = jnp.einsum('sab,sbf->saf', tile_blocks.astype(jnp.float32), gathered.astype(jnp.float32))
        indicator_matrix = ((rows_here[None, :] == row_ids[:, None]) & is_live[None, :]).astype(jnp.float32)
        partial_block_sum = jnp.einsum('rs,saf->raf', indicator_matrix, block_products, precision=lax.Precision.HIGHEST)
        return totals.at[row_part].add(partial_block_sum)
    totals = lax.fori_loop(0, N_ROW * N_COL, forward_block_pass, jnp.zeros((N_ROW, ROW_BLOCKS, BLOCK, feature_width), jnp.float32))
    summed = totals.reshape(nodes_all, feature_width)
    shifted = summed + bias_vector.astype(jnp.float32)
    output = jax.nn.silu(shifted).astype(jnp.bfloat16)
    slope_term = (cotangent.astype(jnp.float32) * silu_slope(shifted)).astype(jnp.bfloat16)
    row_parts = slope_term.reshape(N_ROW, ROW_BLOCKS, BLOCK, feature_width)

    def backward_tile(tile_index, totals):
        row_part = (tile_index // N_COL).astype(jnp.int32)
        col_part = (tile_index % N_COL).astype(jnp.int32)
        grads_here = lax.dynamic_index_in_dim(row_parts, row_part, 0, keepdims=False)
        tile_blocks = adjacency[row_part, col_part]
        rows_here = block_rows[row_part, col_part]
        cols_here = block_cols[row_part, col_part]
        is_live = slot_ids < counts[row_part, col_part]
        gathered = jnp.take(grads_here, rows_here, axis=0)
        block_products = jnp.einsum('sab,saf->sbf', tile_blocks.astype(jnp.float32), gathered.astype(jnp.float32))
        indicator_matrix = ((cols_here[None, :] == col_ids[:, None]) & is_live[None, :]).astype(jnp.float32)
        partial_block_sum = jnp.einsum('ox,xlj->olj', indicator_matrix, block_products, precision=lax.Precision.HIGHEST)
        return totals.at[col_part].add(partial_block_sum)
    back_totals = lax.fori_loop(0, N_ROW * N_COL, backward_tile, jnp.zeros((N_COL, COL_BLOCKS, BLOCK, feature_width), jnp.float32))
    back_totals = back_totals.reshape(N_COL, N_ROW, NODE_DEV, feature_width).transpose(1, 0, 2, 3)
    grad_hidden = back_totals.reshape(nodes_all, feature_width).astype(jnp.bfloat16)
    grad_x = lax.dot_general(grad_hidden, weight, (((1,), (1,)), ((), ())), preferred_element_type=jnp.float32).astype(jnp.bfloat16)
    grad_w = lax.dot_general(features_in, grad_hidden, (((0,), (0,)), ((), ())), preferred_element_type=jnp.float32) * (1.0 / math.sqrt(nodes_all))
    return (output, grad_x, grad_w)
```

```python
import functools
import math

import jax
import jax.numpy as jnp
from jax import lax
from jax.experimental import pallas as pl
from jax.experimental.pallas import tpu as pltpu
from jax.sharding import PartitionSpec as P

bf16 = jnp.bfloat16
f32 = jnp.float32

group = 4
chunk = 32
buffers = 4
z_cols, x_cols = 2, 4


def xor_pairs(size, mask):
    return [(index, index ^ mask) for index in range(size)]


def row_swap(value, mask):
    return lax.ppermute(value, "row", xor_pairs(16, mask))


def col_swap(value, mask):
    return lax.ppermute(value, "col", xor_pairs(8, mask))


def slot_plan(target, source, live, target_total, source_total, position_total):
    slot_total = target.shape[0]
    slots = jnp.arange(slot_total, dtype=jnp.int32)
    target = jnp.where(live, target, target_total)
    targets = jnp.arange(target_total, dtype=jnp.int32)
    member = target[None, :] == targets[:, None]
    sizes = jnp.sum(member.astype(jnp.int32), axis=1)
    padded = ((sizes + group - 1) >> 2) << 2
    ends = jnp.sum(jnp.where(targets[None, :] <= targets[:, None], padded[None, :], 0), axis=1)
    starts = ends - padded
    same_before = (target[None, :] == target[:, None]) & (slots[None, :] < slots[:, None])
    ranks = jnp.sum(same_before.astype(jnp.int32), axis=1)
    position = jnp.sum(jnp.where(member, starts[:, None], 0), axis=0) + ranks
    position = jnp.where(live, position, -1)
    positions = jnp.arange(position_total, dtype=jnp.int32)
    hit = position[None, :] == positions[:, None]
    entry = slots * 128 + source - source_total
    entries = jnp.sum(jnp.where(hit, entry[None, :], 0), axis=1) + source_total
    first = jnp.arange(position_total // group, dtype=jnp.int32) * group
    group_targets = jnp.sum((ends[None, :] <= first[:, None]).astype(jnp.int32), axis=1)
    chunks = (ends[-1:] + chunk - 1) // chunk
    return jnp.concatenate([entries, group_targets, chunks])


def spmm_kernel(piece_total, position_total, source_total, target_total, transposed, *refs):
    plan, blocks = refs[:2]
    pieces = refs[2 : 2 + piece_total]
    outs = refs[2 + piece_total : -5]
    held, source, total, chunk_sems, piece_sems = refs[-5:]
    chunk_total = plan[position_total + position_total // group]

    def fetch(index):
        place = lax.rem(index, buffers)

        def some(step, carry):
            for member in range(8):
                at = step * 8 + member
                slot = plan[index * chunk + at] >> 7
                pltpu.make_async_copy(
                    blocks.at[slot], held.at[place, at], chunk_sems.at[place]
                ).start()
            return carry

        lax.fori_loop(0, chunk // 8, some, 0)

    piece_copies = [
        pltpu.make_async_copy(piece, source.at[pl.ds(4 * index, 4)], piece_sems.at[index])
        for index, piece in enumerate(pieces)
    ]
    for index in range(buffers - 1):

        @pl.when(index < chunk_total)
        def _():
            fetch(index)

        if index == 0:
            for copy in piece_copies:
                copy.start()

    total[...] = jnp.zeros_like(total)
    source[source_total] = jnp.zeros(source.shape[1:], source.dtype)
    for copy in piece_copies:
        copy.wait()

    def chunk_step(index, carry):
        @pl.when(index + buffers - 1 < chunk_total)
        def _():
            fetch(index + buffers - 1)

        place = lax.rem(index, buffers)
        pltpu.make_async_copy(
            blocks.at[pl.ds(0, chunk)], held.at[place], chunk_sems.at[place]
        ).wait()
        for member in range(chunk // group):
            first = member * group
            target = plan[position_total + index * (chunk // group) + member]
            right = jnp.concatenate(
                [source[plan[index * chunk + first + q] & 127] for q in range(group)], axis=0
            )
            left = [held[place, first + q] for q in range(group)]
            if transposed:
                product = lax.dot_general(
                    jnp.concatenate(left, axis=0),
                    right,
                    (((0,), (0,)), ((), ())),
                    preferred_element_type=f32,
                )
            else:
                product = jnp.dot(
                    jnp.concatenate(left, axis=1), right, preferred_element_type=f32
                )
            total[target] += product
        return carry

    lax.fori_loop(0, chunk_total, chunk_step, 0)
    done = 0
    for out in outs:
        count = math.prod(out.shape[:-2])
        out[...] = total[done : done + count].astype(out.dtype).reshape(out.shape)
        done += count


def spmm(plan, blocks, pieces, target_total, position_total, out_shapes, transposed):
    piece_total = len(pieces)
    source_total = 4 * piece_total
    width = pieces[0].shape[-1]
    any_space = pl.BlockSpec(memory_space=pl.ANY)
    return pl.pallas_call(
        functools.partial(
            spmm_kernel, piece_total, position_total, source_total, target_total, transposed
        ),
        out_shape=[jax.ShapeDtypeStruct(shape, bf16) for shape in out_shapes],
        in_specs=[pl.BlockSpec(memory_space=pltpu.SMEM)] + [any_space] * (1 + piece_total),
        out_specs=[pl.BlockSpec(memory_space=pltpu.VMEM)] * len(out_shapes),
        scratch_shapes=[
            pltpu.VMEM((buffers, chunk, 128, 128), bf16),
            pltpu.VMEM((source_total + 1, 128, width), bf16),
            pltpu.VMEM((target_total + 1, 128, width), f32),
            pltpu.SemaphoreType.DMA((buffers,)),
            pltpu.SemaphoreType.DMA((piece_total,)),
        ],
        compiler_params=pltpu.CompilerParams(vmem_limit_bytes=48 << 20),
        cost_estimate=pl.CostEstimate(
            flops=2 * 512 * 128 * 128 * width, bytes_accessed=24 << 20, transcendentals=0
        ),
    )(plan, blocks, *pieces)


def node_kernel(p0, p1, p2, p3, p4, weight, bias, cotangent, output, sent, weight_grad):
    sums = p0[...].astype(f32)
    for part in (p1, p2, p3, p4):
        sums += part[...].astype(f32)
    aggregated = sums.reshape(output.shape).astype(bf16)
    shifted = jnp.dot(aggregated, weight[...], preferred_element_type=f32) + bias[...]
    sigmoid = jax.nn.sigmoid(shifted)
    output[...] = (shifted * sigmoid).astype(bf16)
    slope = sigmoid * (1.0 + shifted * (1.0 - sigmoid))
    slope_term = (cotangent[...].astype(f32) * slope).astype(bf16)
    sent[...] = lax.dot_general(
        slope_term, weight[...], (((1,), (1,)), ((), ())), preferred_element_type=f32
    ).astype(bf16).reshape(sent.shape)
    weight_grad[...] = lax.dot_general(
        aggregated, slope_term, (((0,), (0,)), ((), ())), preferred_element_type=f32
    )


def add_up(*parts):
    sums = parts[0].astype(f32)
    for part in parts[1:]:
        sums = sums + part.astype(f32)
    return sums


def per_device(
    features_in, weight, bias_vector, cotangent, adjacency, block_rows, block_cols, counts
):
    node_dev, width = features_in.shape
    piece = (4, 128, width)
    blocks = adjacency[0, 0]
    rows_here = block_rows[0, 0]
    cols_here = block_cols[0, 0]
    slot_total = rows_here.shape[0]
    live = jnp.arange(slot_total, dtype=jnp.int32) < counts[0, 0]
    row_index = lax.axis_index("row")
    col_index = lax.axis_index("col")

    row_place = (((col_index ^ (rows_here >> 2)) << 2) | (rows_here & 3)).astype(jnp.int32)
    partner = row_index ^ (cols_here >> 2)
    col_place = ((((partner & 1) << 3) | (partner >> 1)) << 2) | (cols_here & 3)
    forward_plan = slot_plan(row_place, col_place, live, 32, 64, slot_total + 96)
    backward_plan = slot_plan(col_place, row_place, live, 64, 32, slot_total + 192)

    own = features_in.reshape(piece)
    beside = row_swap(own, 2)
    near = [own, beside]
    for y in (1, 3, 2):
        near += [row_swap(own, 4 * y), row_swap(beside, 4 * y)]
    near = near[:2] + near[2:4] + near[6:8] + near[4:6]
    gathered = near + [row_swap(part, 1) for part in near]

    parts = spmm(forward_plan, blocks, gathered, 32, slot_total + 96, [piece] * 8, False)
    across = [col_swap(parts[4 + x], x) for x in (1, 3, 2)]
    here = [col_swap(parts[x], x) for x in (1, 3, 2)]
    across_sum = add_up(parts[4], *across).astype(bf16)
    from_across = col_swap(across_sum, 4)

    output, sent, weight_grad = pl.pallas_call(
        node_kernel,
        out_shape=[
            jax.ShapeDtypeStruct((node_dev, width), bf16),
            jax.ShapeDtypeStruct(piece, bf16),
            jax.ShapeDtypeStruct((width, width), f32),
        ],
        compiler_params=pltpu.CompilerParams(vmem_limit_bytes=32 << 20),
    )(parts[0], *here, from_across, weight, bias_vector[None, :], cotangent)

    beside = col_swap(sent, 4)
    x_order = (1, 3, 2)
    from_here = {x: col_swap(sent, x) for x in x_order}
    from_there = {x: col_swap(beside, x) for x in x_order}
    spread = [sent] + [from_here[x] for x in (1, 2, 3)]
    spread += [beside] + [from_there[x] for x in (1, 2, 3)]

    device_total = 128
    scatter = lax.all_to_all(
        weight_grad.reshape(device_total, -1), ("row", "col"), 0, 0, tiled=True
    )
    scattered = jnp.sum(scatter, axis=0, keepdims=True) * (
        1.0 / math.sqrt(node_dev * device_total)
    )
    grad_w = lax.all_to_all(
        jnp.broadcast_to(scattered, scatter.shape), ("row", "col"), 0, 0, tiled=True
    ).reshape(width, width)

    halves = spmm(
        backward_plan, blocks, spread, 64, slot_total + 192, [(8,) + piece] * 2, True
    )
    mine, theirs = halves
    swapped = row_swap(theirs, 1)
    summed = [add_up(mine[index], swapped[index]).astype(bf16) for index in range(8)]
    across = [row_swap(summed[2 * y + 1], 4 * y) for y in (1, 3, 2)]
    here = [row_swap(summed[2 * y], 4 * y) for y in (1, 3, 2)]
    across_sum = add_up(summed[1], *across).astype(bf16)
    from_across = row_swap(across_sum, 2)
    grad_x = add_up(summed[0], *here, from_across).astype(bf16).reshape(node_dev, width)
    return (output, grad_x, grad_w)


def solution(mesh):
    in_specs = (
        P(("row", "col"), None),
        P(),
        P(),
        P(("row", "col"), None),
        P("row", "col", None, None, None),
        P("row", "col", None),
        P("row", "col", None),
        P("row", "col"),
    )
    out_specs = (P(("row", "col"), None), P(("row", "col"), None), P())
    return jax.shard_map(
        per_device, mesh=mesh, in_specs=in_specs, out_specs=out_specs, check_vma=False
    )
```

```python
import functools
import math

import jax
import jax.numpy as jnp
from jax import lax
from jax.experimental import pallas as pl
from jax.experimental.pallas import tpu as pltpu
from jax.sharding import PartitionSpec as P

bf16 = jnp.bfloat16
f32 = jnp.float32

group = 4
chunk = 32
buffers = 4
z_cols, x_cols = 2, 4


def xor_pairs(size, mask):
    return [(index, index ^ mask) for index in range(size)]


def row_swap(value, mask):
    return lax.ppermute(value, "row", xor_pairs(16, mask))


def col_swap(value, mask):
    return lax.ppermute(value, "col", xor_pairs(8, mask))


def slot_plan(target, source, live, target_total, source_total, position_total):
    slot_total = target.shape[0]
    slots = jnp.arange(slot_total, dtype=jnp.int32)
    target = jnp.where(live, target, target_total)
    targets = jnp.arange(target_total, dtype=jnp.int32)
    member = target[None, :] == targets[:, None]
    sizes = jnp.sum(member.astype(jnp.int32), axis=1)
    padded = ((sizes + group - 1) >> 2) << 2
    ends = jnp.sum(jnp.where(targets[None, :] <= targets[:, None], padded[None, :], 0), axis=1)
    starts = ends - padded
    same_before = (target[None, :] == target[:, None]) & (slots[None, :] < slots[:, None])
    ranks = jnp.sum(same_before.astype(jnp.int32), axis=1)
    position = jnp.sum(jnp.where(member, starts[:, None], 0), axis=0) + ranks
    position = jnp.where(live, position, -1)
    positions = jnp.arange(position_total, dtype=jnp.int32)
    hit = position[None, :] == positions[:, None]
    entry = slots * 128 + source - source_total
    entries = jnp.sum(jnp.where(hit, entry[None, :], 0), axis=1) + source_total
    first = jnp.arange(position_total // group, dtype=jnp.int32) * group
    group_targets = jnp.sum((ends[None, :] <= first[:, None]).astype(jnp.int32), axis=1)
    chunks = (jnp.sum(padded, keepdims=True) + chunk - 1) // chunk
    return jnp.concatenate([entries, group_targets, chunks])


def spmm_kernel(piece_total, position_total, source_total, target_total, transposed, *refs):
    plan, blocks = refs[:2]
    pieces = refs[2 : 2 + piece_total]
    outs = refs[2 + piece_total : -5]
    held, source, total, chunk_sems, piece_sems = refs[-5:]
    chunk_total = plan[position_total + position_total // group]

    def fetch(index):
        place = lax.rem(index, buffers)

        def some(step, carry):
            for member in range(8):
                at = step * 8 + member
                slot = plan[index * chunk + at] >> 7
                pltpu.make_async_copy(
                    blocks.at[slot], held.at[place, at], chunk_sems.at[place]
                ).start()
            return carry

        lax.fori_loop(0, chunk // 8, some, 0)

    piece_copies = [
        pltpu.make_async_copy(piece, source.at[pl.ds(4 * index, 4)], piece_sems.at[index])
        for index, piece in enumerate(pieces)
    ]
    for index in range(buffers - 1):

        @pl.when(index < chunk_total)
        def _():
            fetch(index)

        if index == 0:
            for copy in piece_copies:
                copy.start()

    total[...] = jnp.zeros_like(total)
    source[source_total] = jnp.zeros(source.shape[1:], source.dtype)
    for copy in piece_copies:
        copy.wait()

    def chunk_step(index, carry):
        @pl.when(index + buffers - 1 < chunk_total)
        def _():
            fetch(index + buffers - 1)

        place = lax.rem(index, buffers)
        pltpu.make_async_copy(
            blocks.at[pl.ds(0, chunk)], held.at[place], chunk_sems.at[place]
        ).wait()
        for member in range(chunk // group):
            first = member * group
            target = plan[position_total + index * (chunk // group) + member]
            right = jnp.concatenate(
                [source[plan[index * chunk + first + q] & 127] for q in range(group)], axis=0
            )
            left = [held[place, first + q] for q in range(group)]
            if transposed:
                product = lax.dot_general(
                    jnp.concatenate(left, axis=0),
                    right,
                    (((0,), (0,)), ((), ())),
                    preferred_element_type=f32,
                )
            else:
                product = jnp.dot(
                    jnp.concatenate(left, axis=1), right, preferred_element_type=f32
                )
            total[target] += product
        return carry

    lax.fori_loop(0, chunk_total, chunk_step, 0)
    done = 0
    for out in outs:
        count = math.prod(out.shape[:-2])
        out[...] = total[done : done + count].astype(out.dtype).reshape(out.shape)
        done += count


def spmm(plan, blocks, pieces, target_total, position_total, out_shapes, transposed, grant):
    piece_total = len(pieces)
    source_total = 4 * piece_total
    width = pieces[0].shape[-1]
    any_space = pl.BlockSpec(memory_space=pl.ANY)
    return pl.pallas_call(
        functools.partial(
            spmm_kernel, piece_total, position_total, source_total, target_total, transposed
        ),
        out_shape=[jax.ShapeDtypeStruct(shape, bf16) for shape in out_shapes],
        in_specs=[pl.BlockSpec(memory_space=pltpu.SMEM)] + [any_space] * (1 + piece_total),
        out_specs=[pl.BlockSpec(memory_space=pltpu.VMEM)] * len(out_shapes),
        scratch_shapes=[
            pltpu.VMEM((buffers, chunk, 128, 128), bf16),
            pltpu.VMEM((source_total + 1, 128, width), bf16),
            pltpu.VMEM((target_total + 1, 128, width), f32),
            pltpu.SemaphoreType.DMA((buffers,)),
            pltpu.SemaphoreType.DMA((piece_total,)),
        ],
        compiler_params=pltpu.CompilerParams(vmem_limit_bytes=grant << 20),
        cost_estimate=pl.CostEstimate(
            flops=2 * 512 * 128 * 128 * width, bytes_accessed=24 << 20, transcendentals=0
        ),
    )(plan, blocks, *pieces)


def node_kernel(p0, p1, p2, p3, p4, weight, bias, cotangent, output, sent, weight_grad):
    sums = p0[...].astype(f32)
    for part in (p1, p2, p3, p4):
        sums += part[...].astype(f32)
    aggregated = sums.reshape(output.shape).astype(bf16)
    shifted = jnp.dot(aggregated, weight[...], preferred_element_type=f32) + bias[...]
    sigmoid = jax.nn.sigmoid(shifted)
    output[...] = (shifted * sigmoid).astype(bf16)
    slope = sigmoid * (1.0 + shifted * (1.0 - sigmoid))
    slope_term = (cotangent[...].astype(f32) * slope).astype(bf16)
    sent[...] = lax.dot_general(
        slope_term, weight[...], (((1,), (1,)), ((), ())), preferred_element_type=f32
    ).astype(bf16).reshape(sent.shape)
    weight_grad[...] = lax.dot_general(
        aggregated, slope_term, (((0,), (0,)), ((), ())), preferred_element_type=f32
    )


def add_up(*parts):
    sums = parts[0].astype(f32)
    for part in parts[1:]:
        sums = sums + part.astype(f32)
    return sums


def together(*values):
    return lax.optimization_barrier(values)


def gather_near(own, swap, follow=(), state=None):
    two, beside = swap(own, 2, 0), swap(own, 0, 1)
    if follow:
        own, two, beside, state = together(own, two, beside, follow[0](state))
    one, three = swap(own, 1, 0), swap(own, 3, 0)
    second = [swap(beside, 1, 0), swap(beside, 3, 0), swap(two, 0, 1)]
    if follow:
        *second, one, three, state = together(*second, one, three, follow[1](state))
    return [[own, one, two, three], [beside, second[0], second[2], second[1]]], state


def scatter_near(parts, swap, follow=(), state=None):
    here, there = parts
    opposite = swap(there[2], 0, 1)
    edges = [swap(there[ring], ring, 0) for ring in (1, 3)]
    if follow:
        state = follow[0](state)
    side = add_up(there[0], *edges).astype(bf16)
    corner = add_up(here[2], opposite).astype(bf16)
    one, three = here[1], here[3]
    if follow:
        side, corner, one, three, state = together(side, corner, one, three, state)
    near = [swap(one, 1, 0), swap(three, 3, 0)]
    beside, far = swap(side, 0, 1), swap(corner, 2, 0)
    if follow:
        state = follow[1](state)
    return [here[0], *near, beside, far], state


def ring_sum(value, swaps):
    rounded = value.astype(bf16)
    one, two, three = [swap(rounded).astype(f32) for swap in swaps]
    return (rounded.astype(f32) + one) + (two + three)


def all_swap(value, row_mask, col_mask):
    pairs = [(index, index ^ (8 * row_mask + col_mask)) for index in range(128)]
    return lax.ppermute(value, ("row", "col"), pairs)


def cut(array, part, count):
    return lax.dynamic_slice_in_dim(array, part * count, count, 0)


def per_device(
    features_in, weight, bias_vector, cotangent, adjacency, block_rows, block_cols, counts
):
    node_dev, width = features_in.shape
    piece = (4, 128, width)
    blocks = adjacency[0, 0]
    rows_here = block_rows[0, 0]
    cols_here = block_cols[0, 0]
    slot_total = rows_here.shape[0]
    live = jnp.arange(slot_total, dtype=jnp.int32) < counts[0, 0]
    row_index = lax.axis_index("row")
    col_index = lax.axis_index("col")

    row_place = (((col_index ^ (rows_here >> 2)) << 2) | (rows_here & 3)).astype(jnp.int32)
    partner = row_index ^ (cols_here >> 2)
    col_place = ((((partner & 1) << 3) | (partner >> 1)) << 2) | (cols_here & 3)
    forward_plan = slot_plan(row_place, col_place, live, 32, 64, slot_total + 96)
    backward_plan = slot_plan(col_place, row_place, live, 64, 32, slot_total + 192)

    own = features_in.reshape(piece)
    near, _ = gather_near(own, lambda value, ring, z: row_swap(value, 4 * ring + 2 * z))
    near = [near[z][ring] for ring in range(4) for z in range(2)]
    gathered = near + [row_swap(part, 1) for part in near]

    parts = spmm(forward_plan, blocks, gathered, 32, slot_total + 96, [piece] * 8, False, 48)
    terms, _ = scatter_near(
        [parts[:4], parts[4:]], lambda value, ring, z: col_swap(value, ring + 4 * z)
    )

    output, sent, weight_grad = pl.pallas_call(
        node_kernel,
        out_shape=[
            jax.ShapeDtypeStruct((node_dev, width), bf16),
            jax.ShapeDtypeStruct(piece, bf16),
            jax.ShapeDtypeStruct((width, width), f32),
        ],
        compiler_params=pltpu.CompilerParams(vmem_limit_bytes=32 << 20),
    )(*terms, weight, bias_vector[None, :], cotangent)

    core = row_index & 1
    count = width // 2
    spread, half = gather_near(
        sent,
        lambda value, ring, z: col_swap(value, ring + 4 * z),
        (
            lambda full: cut(full, core, count) + row_swap(cut(full, core ^ 1, count), 1),
            lambda part: ring_sum(part, [lambda v, k=k: row_swap(v, 4 * k) for k in (1, 2, 3)]),
        ),
        weight_grad,
    )

    mine, theirs = spmm(
        backward_plan,
        blocks,
        spread[0] + spread[1],
        64,
        slot_total + 192,
        [(8,) + piece] * 2,
        True,
        42,
    )
    half = ring_sum(
        half, [lambda v, m=m: all_swap(v, *m) for m in ((2, 0), (0, 4), (2, 4))]
    )
    swapped, half = together(row_swap(theirs, 1), half)
    summed = [add_up(mine[index], swapped[index]).astype(bf16) for index in range(8)]
    terms, other = scatter_near(
        [summed[0::2], summed[1::2]],
        lambda value, ring, z: row_swap(value, 4 * ring + 2 * z),
        (
            lambda part: ring_sum(part, [lambda v, k=k: col_swap(v, k) for k in (1, 2, 3)]),
            lambda part: (part, row_swap(part, 1)),
        ),
        half,
    )
    half, other = [part * (1.0 / math.sqrt(node_dev * 128)) for part in other]
    grad_w = jnp.concatenate(
        [jnp.where(core == 0, half, other), jnp.where(core == 0, other, half)], axis=0
    )
    grad_x = add_up(*terms).astype(bf16).reshape(node_dev, width)
    return (output, grad_x, grad_w)


def solution(mesh):
    in_specs = (
        P(("row", "col"), None),
        P(),
        P(),
        P(("row", "col"), None),
        P("row", "col", None, None, None),
        P("row", "col", None),
        P("row", "col", None),
        P("row", "col"),
    )
    out_specs = (P(("row", "col"), None), P(("row", "col"), None), P())
    return jax.shard_map(
        per_device, mesh=mesh, in_specs=in_specs, out_specs=out_specs, check_vma=False
    )
```

```python
import functools
import math

import jax
import jax.numpy as jnp
from jax import lax
from jax.experimental import pallas as pl
from jax.experimental.pallas import tpu as pltpu
from jax.sharding import PartitionSpec as P

bf16 = jnp.bfloat16
f32 = jnp.float32

group = 4
chunk = 32
buffers = 4
z_cols, x_cols = 2, 4


def xor_pairs(size, mask):
    return [(index, index ^ mask) for index in range(size)]


def row_swap(value, mask):
    return lax.ppermute(value, "row", xor_pairs(16, mask))


def col_swap(value, mask):
    return lax.ppermute(value, "col", xor_pairs(8, mask))


def slot_plan(target, source, live, target_total, source_total, position_total):
    slot_total = target.shape[0]
    slots = jnp.arange(slot_total, dtype=jnp.int32)
    target = jnp.where(live, target, target_total)
    targets = jnp.arange(target_total, dtype=jnp.int32)
    member = target[None, :] == targets[:, None]
    sizes = jnp.sum(member.astype(jnp.int32), axis=1)
    padded = ((sizes + group - 1) >> 2) << 2
    ends = jnp.sum(jnp.where(targets[None, :] <= targets[:, None], padded[None, :], 0), axis=1)
    starts = ends - padded
    same_before = (target[None, :] == target[:, None]) & (slots[None, :] < slots[:, None])
    ranks = jnp.sum(same_before.astype(jnp.int32), axis=1)
    position = jnp.sum(jnp.where(member, starts[:, None], 0), axis=0) + ranks
    position = jnp.where(live, position, -1)
    positions = jnp.arange(position_total, dtype=jnp.int32)
    hit = position[None, :] == positions[:, None]
    entry = slots * 128 + source - source_total
    entries = jnp.sum(jnp.where(hit, entry[None, :], 0), axis=1) + source_total
    first = jnp.arange(position_total // group, dtype=jnp.int32) * group
    group_targets = jnp.sum((ends[None, :] <= first[:, None]).astype(jnp.int32), axis=1)
    chunks = (jnp.sum(padded, keepdims=True) + chunk - 1) // chunk
    return jnp.concatenate([entries, group_targets, chunks])


def spmm_kernel(piece_total, position_total, source_total, target_total, transposed, *refs):
    plan, blocks = refs[:2]
    pieces = refs[2 : 2 + piece_total]
    outs = refs[2 + piece_total : -5]
    held, source, total, chunk_sems, piece_sems = refs[-5:]
    chunk_total = plan[position_total + position_total // group]

    def fetch(index):
        place = lax.rem(index, buffers)

        def some(step, carry):
            for member in range(8):
                at = step * 8 + member
                slot = plan[index * chunk + at] >> 7
                pltpu.make_async_copy(
                    blocks.at[slot], held.at[place, at], chunk_sems.at[place]
                ).start()
            return carry

        lax.fori_loop(0, chunk // 8, some, 0)

    piece_copies = [
        pltpu.make_async_copy(piece, source.at[pl.ds(4 * index, 4)], piece_sems.at[index])
        for index, piece in enumerate(pieces)
    ]
    for index in range(buffers - 1):

        @pl.when(index < chunk_total)
        def _():
            fetch(index)

        if index == 0:
            for copy in piece_copies:
                copy.start()

    total[...] = jnp.zeros_like(total)
    source[source_total] = jnp.zeros(source.shape[1:], source.dtype)
    for copy in piece_copies:
        copy.wait()

    def chunk_step(index, carry):
        @pl.when(index + buffers - 1 < chunk_total)
        def _():
            fetch(index + buffers - 1)

        place = lax.rem(index, buffers)
        pltpu.make_async_copy(
            blocks.at[pl.ds(0, chunk)], held.at[place], chunk_sems.at[place]
        ).wait()
        for member in range(chunk // group):
            first = member * group
            target = plan[position_total + index * (chunk // group) + member]
            right = jnp.concatenate(
                [source[plan[index * chunk + first + q] & 127] for q in range(group)], axis=0
            )
            left = [held[place, first + q] for q in range(group)]
            if transposed:
                product = lax.dot_general(
                    jnp.concatenate(left, axis=0),
                    right,
                    (((0,), (0,)), ((), ())),
                    preferred_element_type=f32,
                )
            else:
                product = jnp.dot(
                    jnp.concatenate(left, axis=1), right, preferred_element_type=f32
                )
            total[target] += product
        return carry

    lax.fori_loop(0, chunk_total, chunk_step, 0)
    done = 0
    for out in outs:
        count = math.prod(out.shape[:-2])
        out[...] = total[done : done + count].astype(out.dtype).reshape(out.shape)
        done += count


def spmm(plan, blocks, pieces, target_total, position_total, out_shapes, transposed, grant):
    piece_total = len(pieces)
    source_total = 4 * piece_total
    width = pieces[0].shape[-1]
    any_space = pl.BlockSpec(memory_space=pl.ANY)
    return pl.pallas_call(
        functools.partial(
            spmm_kernel, piece_total, position_total, source_total, target_total, transposed
        ),
        out_shape=[jax.ShapeDtypeStruct(shape, bf16) for shape in out_shapes],
        in_specs=[pl.BlockSpec(memory_space=pltpu.SMEM)] + [any_space] * (1 + piece_total),
        out_specs=[pl.BlockSpec(memory_space=pltpu.VMEM)] * len(out_shapes),
        scratch_shapes=[
            pltpu.VMEM((buffers, chunk, 128, 128), bf16),
            pltpu.VMEM((source_total + 1, 128, width), bf16),
            pltpu.VMEM((target_total + 1, 128, width), f32),
            pltpu.SemaphoreType.DMA((buffers,)),
            pltpu.SemaphoreType.DMA((piece_total,)),
        ],
        compiler_params=pltpu.CompilerParams(vmem_limit_bytes=grant << 20),
        cost_estimate=pl.CostEstimate(
            flops=2 * 512 * 128 * 128 * width, bytes_accessed=24 << 20, transcendentals=0
        ),
    )(plan, blocks, *pieces)


def node_kernel(p0, p1, p2, p3, p4, weight, bias, cotangent, output, sent, weight_grad):
    sums = p0[...].astype(f32)
    for part in (p1, p2, p3, p4):
        sums += part[...].astype(f32)
    aggregated = sums.reshape(output.shape).astype(bf16)
    shifted = jnp.dot(aggregated, weight[...], preferred_element_type=f32) + bias[...]
    sigmoid = jax.nn.sigmoid(shifted)
    output[...] = (shifted * sigmoid).astype(bf16)
    slope = sigmoid * (1.0 + shifted * (1.0 - sigmoid))
    slope_term = (cotangent[...].astype(f32) * slope).astype(bf16)
    sent[...] = lax.dot_general(
        slope_term, weight[...], (((1,), (1,)), ((), ())), preferred_element_type=f32
    ).astype(bf16).reshape(sent.shape)
    weight_grad[...] = lax.dot_general(
        aggregated, slope_term, (((0,), (0,)), ((), ())), preferred_element_type=f32
    )


def add_up(*parts):
    sums = parts[0].astype(f32)
    for part in parts[1:]:
        sums = sums + part.astype(f32)
    return sums


def together(*values):
    return lax.optimization_barrier(values)


def gather_near(own, swap, follow=(), state=None):
    two, beside = swap(own, 2, 0), swap(own, 0, 1)
    if follow:
        own, two, beside, state = together(own, two, beside, follow[0](state))
    one, three = swap(own, 1, 0), swap(own, 3, 0)
    second = [swap(beside, 1, 0), swap(beside, 3, 0), swap(two, 0, 1)]
    if follow:
        *second, one, three, state = together(*second, one, three, follow[1](state))
    return [[own, one, two, three], [beside, second[0], second[2], second[1]]], state


def scatter_near(parts, swap, follow=(), state=None):
    here, there = parts
    opposite = swap(there[2], 0, 1)
    edges = [swap(there[ring], ring, 0) for ring in (1, 3)]
    if follow:
        state = follow[0](state)
    side = add_up(there[0], *edges).astype(bf16)
    corner = add_up(here[2], opposite).astype(bf16)
    one, three = here[1], here[3]
    if follow:
        side, corner, one, three, state = together(side, corner, one, three, state)
    near = [swap(one, 1, 0), swap(three, 3, 0)]
    beside, far = swap(side, 0, 1), swap(corner, 2, 0)
    if follow:
        state = follow[1](state)
    return [here[0], *near, beside, far], state


def ring_sum(value, swaps):
    rounded = value.astype(bf16)
    one, two, three = [swap(rounded).astype(f32) for swap in swaps]
    return (rounded.astype(f32) + one) + (two + three)


def all_swap(value, row_mask, col_mask):
    pairs = [(index, index ^ (8 * row_mask + col_mask)) for index in range(128)]
    return lax.ppermute(value, ("row", "col"), pairs)


def per_device(
    features_in, weight, bias_vector, cotangent, adjacency, block_rows, block_cols, counts
):
    node_dev, width = features_in.shape
    piece = (4, 128, width)
    blocks = adjacency[0, 0]
    rows_here = block_rows[0, 0]
    cols_here = block_cols[0, 0]
    slot_total = rows_here.shape[0]
    live = jnp.arange(slot_total, dtype=jnp.int32) < counts[0, 0]
    row_index = lax.axis_index("row")
    col_index = lax.axis_index("col")

    row_place = (((col_index ^ (rows_here >> 2)) << 2) | (rows_here & 3)).astype(jnp.int32)
    partner = row_index ^ (cols_here >> 2)
    col_place = ((((partner & 1) << 3) | (partner >> 1)) << 2) | (cols_here & 3)
    forward_plan = slot_plan(row_place, col_place, live, 32, 64, slot_total + 96)
    backward_plan = slot_plan(col_place, row_place, live, 64, 32, slot_total + 192)

    own = features_in.reshape(piece)
    near, _ = gather_near(own, lambda value, ring, z: row_swap(value, 4 * ring + 2 * z))
    near = [near[z][ring] for ring in range(4) for z in range(2)]
    gathered = near + [row_swap(part, 1) for part in near]

    parts = spmm(forward_plan, blocks, gathered, 32, slot_total + 96, [piece] * 8, False, 48)
    terms, _ = scatter_near(
        [parts[:4], parts[4:]], lambda value, ring, z: col_swap(value, ring + 4 * z)
    )

    output, sent, weight_grad = pl.pallas_call(
        node_kernel,
        out_shape=[
            jax.ShapeDtypeStruct((node_dev, width), bf16),
            jax.ShapeDtypeStruct(piece, bf16),
            jax.ShapeDtypeStruct((width, width), f32),
        ],
        compiler_params=pltpu.CompilerParams(vmem_limit_bytes=32 << 20),
    )(*terms, weight, bias_vector[None, :], cotangent)

    spread, weight_sum = gather_near(
        sent,
        lambda value, ring, z: col_swap(value, ring + 4 * z),
        (
            lambda part: ring_sum(part, [lambda v, k=k: row_swap(v, 4 * k) for k in (1, 2, 3)]),
            lambda part: ring_sum(
                part, [lambda v, m=m: all_swap(v, *m) for m in ((2, 0), (0, 4), (2, 4))]
            ),
        ),
        weight_grad,
    )

    mine, theirs = spmm(
        backward_plan,
        blocks,
        spread[0] + spread[1],
        64,
        slot_total + 192,
        [(8,) + piece] * 2,
        True,
        42,
    )
    rounded = weight_sum.astype(bf16)
    weight_sum = rounded.astype(f32) + row_swap(rounded, 1).astype(f32)
    swapped, weight_sum = together(row_swap(theirs, 1), weight_sum)
    summed = [add_up(mine[index], swapped[index]).astype(bf16) for index in range(8)]
    terms, weight_sum = scatter_near(
        [summed[0::2], summed[1::2]],
        lambda value, ring, z: row_swap(value, 4 * ring + 2 * z),
        (
            lambda part: ring_sum(part, [lambda v, k=k: col_swap(v, k) for k in (1, 2, 3)]),
            lambda part: part,
        ),
        weight_sum,
    )
    grad_w = weight_sum * (1.0 / math.sqrt(node_dev * 128))
    grad_x = add_up(*terms).astype(bf16).reshape(node_dev, width)
    return (output, grad_x, grad_w)


def solution(mesh):
    in_specs = (
        P(("row", "col"), None),
        P(),
        P(),
        P(("row", "col"), None),
        P("row", "col", None, None, None),
        P("row", "col", None),
        P("row", "col", None),
        P("row", "col"),
    )
    out_specs = (P(("row", "col"), None), P(("row", "col"), None), P())
    return jax.shard_map(
        per_device, mesh=mesh, in_specs=in_specs, out_specs=out_specs, check_vma=False
    )
```
